512 devices in a mesh: row: 16 (over x, z_hi, core), col: 32 (over y, z_lo).
Axes of the slice: x: 4, y: 4, z: 16 (z_hi: 2, z_lo: 8; z = z_hi * 8 + z_lo), core: 2. Of those that a mesh axis runs over, the one named last changes fastest.
Arguments:
- anomalies: bfloat16 [128, 131072], P(None, ('col', 'row')), may hold values from -16 to 16
- vectors: bfloat16 [64, 131072], P(None, ('col', 'row')), may hold values from -0.1796875 to 0.1796875
Outputs:
- applied: float32 [64, 65536], P(None, ('row', 'col'))
The draws below stay inside these ranges and needn't reach their ends.
All inputs are finite; a program needn't handle non-finite values.
Results may differ from the reference program's by a relative error of at most 0.0035.
Values may be sent and summed in bfloat16 or wider, within the bound.
A program may use at most 64 MiB of HBM per device.

```python
import math
import jax
import jax.numpy as jnp
from jax import lax

M = 128
K = 64
NSTATE = 131072
WROWS = 65536


def mixed_columns(key_list, coupling):
    mode_count = 16
    mode_ids = jax.random.randint(key_list[0], (3, NSTATE), 0, mode_count)
    factors = jax.random.normal(key_list[1], (M, mode_count), jnp.float32)
    common_part = jax.random.normal(key_list[2], (M, 1), jnp.float32)
    common = factors + common_part
    signs = (2 * jax.random.randint(key_list[3], (3, NSTATE), 0, 2) - 1).astype(jnp.float32)
    weights = signs * jax.random.uniform(key_list[4], (3, NSTATE), jnp.float32, 0.3, 1.5)
    mixture = weights[0][None, :] * jnp.take(common, mode_ids[0], axis=1)
    mixture = mixture + weights[1][None, :] * jnp.take(common, mode_ids[1], axis=1)
    mixture = mixture + weights[2][None, :] * jnp.take(common, mode_ids[2], axis=1)
    scale_sq = (1.0 + coupling) * (weights[0] * weights[0] + weights[1] * weights[1] + weights[2] * weights[2])
    return mixture / jnp.sqrt(scale_sq)[None, :]


def draw_anomalies(key, part):
    key = jax.random.fold_in(key, 7)
    key_list = jax.random.split(key, 9)
    strength = jax.random.uniform(key_list[5], (NSTATE,), jnp.float32, 0.5, 3.0)
    mixture = mixed_columns(key_list, 1.0)
    noise_part = jax.random.normal(key_list[6], (M, NSTATE), jnp.float32)
    spread = jnp.exp(jax.random.uniform(key_list[7], (NSTATE,), jnp.float32, math.log(0.3), math.log(3.0)))
    values = spread[None, :] * (strength[None, :] * mixture + noise_part) * 0.5
    return jnp.clip(values, -16.0, 16.0).astype(jnp.bfloat16)


def steps_of(rng, extent, cuts, low, largest):
    def one(position, parts):
        draws = jax.random.uniform(jax.random.fold_in(jax.random.fold_in(rng, 6), position), (parts,), jnp.float32, low / len(cuts), largest / len(cuts))
        return jnp.repeat(jnp.exp(draws), extent[position] // parts).reshape((-1,) + (1,) * (len(extent) - position - 1))

    loudness = one(*cuts[0])
    for cut in cuts[1:]:
        loudness = loudness * one(*cut)
    return loudness


def normal_values(rng, shape, scale, reach, pieces=(), kind=jnp.bfloat16):
    level = steps_of(rng, shape, pieces, -0.22, 0.18) if pieces else 1.0
    entries = jax.random.normal(rng, shape, jnp.float32) * scale * level
    return jnp.minimum(jnp.maximum(entries, -reach), reach).astype(kind)


def setup_inputs(seed: int = 0) -> dict:
    streams_of = jax.random.split(jax.random.key(seed), 3)
    anomalies = draw_anomalies(jax.random.fold_in(streams_of[2], 71), 0)
    vectors = normal_values(streams_of[1], (K, NSTATE), 0.03, 0.1796875, ((1, 512),))
    return {"anomalies": anomalies, "vectors": vectors}


def spreads(anomaly_block, inverse):
    wide = anomaly_block.astype(jnp.float32)
    return jnp.sqrt(lax.optimization_barrier(jnp.sum(wide * wide, axis=0)) * inverse + 1e-06)

def localize(row_part, row_spread, col_anom, col_spread, col_vec, inverse):
    cov = lax.dot_general(row_part, col_anom, (((0,), (0,)), ((), ())), preferred_element_type=jnp.float32) * inverse
    corr = cov / (row_spread[:, None] * col_spread[None, :])
    local = (corr * corr * corr * cov).astype(jnp.bfloat16)
    return lax.dot_general(col_vec, local, (((1,), (1,)), ((), ())), preferred_element_type=jnp.float32)

def reference(anomalies, vectors):
    inverse = 1.0 / (M - 1.0)
    spread = spreads(anomalies, inverse)
    row_block = math.gcd(WROWS, 256)
    count = WROWS // row_block
    window = anomalies[:, :WROWS]
    blocks = window.reshape(M, count, row_block).transpose(1, 0, 2)
    spread_blocks = spread[:WROWS].reshape(count, row_block)

    def one_block(inputs_pair):
        return localize(inputs_pair[0], inputs_pair[1], anomalies, spread, vectors, inverse)
    stacked = lax.map(one_block, (blocks, spread_blocks))
    return stacked.transpose(1, 0, 2).reshape(K, WROWS)
```

```python
import jax
import jax.numpy as jnp
from jax import lax
from jax.experimental import pallas as pl
from jax.experimental.pallas import tpu as pltpu
from jax.sharding import PartitionSpec as P

MESH = pl.DeviceIdType.MESH
F32 = jnp.float32
BF16 = jnp.bfloat16
MEMBERS = 128
VECS = 64
INV = 1.0 / (MEMBERS - 1.0)
JROWS = 400
IROWS = 272

ORDER = [
    (0, 0), (1, 0), (3, 0), (0, 1), (0, 3), (2, 0), (0, 2), (1, 1),
    (1, 3), (3, 1), (3, 3), (1, 2), (3, 2), (2, 1), (2, 3), (2, 2),
]
SLOT = {off: n for n, off in enumerate(ORDER)}
EARLY = [(0, 5), (16, 5)]
LATE = [(5, 6), (11, 5), (21, 6), (27, 5)]


def dot(a, b):
    return jnp.dot(a, b, preferred_element_type=F32)


def split_three(c):
    hi = c.astype(BF16).astype(F32)
    rest = c - hi
    mid = rest.astype(BF16).astype(F32)
    return hi, mid, rest - mid


def kernel(a_ref, v_ref, o_ref, jbuf, vbuf, ibuf, imsg, acc, rsm, rsp,
           send_sem, jrecv, irecv, mrecv, precv, local_sem):
    row, col = lax.axis_index("row"), lax.axis_index("col")
    x, zh, core = row // 4, (row // 2) % 2, row % 2
    y, zl = col // 8, col % 8
    z = zh * 8 + zl

    def at(x_, y_, z_, core_):
        return {"row": x_ * 4 + (z_ // 8) * 2 + core_, "col": y_ * 8 + z_ % 8}

    p = x + core * (y - x)
    q = y + core * (x - y)

    def at_pq(p_, q_):
        return at(p_ + core * (q_ - p_), q_ + core * (p_ - q_), z, core)

    sib = at(x, y, z, 1 - core)
    p_up, p_dn = at_pq((p + 1) % 4, q), at_pq((p + 3) % 4, q)
    q_up, q_dn = at_pq(p, (q + 1) % 4), at_pq(p, (q + 3) % 4)
    z_up, z_dn = at(x, y, (z + 1) % 16, core), at(x, y, (z + 15) % 16, core)

    gives = y < 2
    sd = 4 * ((zl // 2) % 2) + 2 * zh + core
    tx, ty, tc = 2 * (y % 2) + zl // 4, x, zl % 2
    same_line = (tx == x) & (ty == y) & (tc == core) & gives
    own_lo, own_hi = same_line & (z == sd), same_line & (z == sd + 8)
    s0 = zl
    gy, gx = x // 2, y
    gzl = (x % 2) * 4 + 2 * (s0 // 4) + core
    gz = 8 * ((s0 % 4) // 2) + gzl
    gc = s0 % 2
    from_self = (gx == x) & (gy == y) & (gz == z) & (gc == core)

    barrier = pltpu.get_barrier_semaphore()
    for dev in (sib, p_up, p_dn, q_up, q_dn, z_up, z_dn):
        pl.semaphore_signal(barrier, inc=1, device_id=dev, device_id_type=MESH)

    @pl.when(jnp.logical_not(from_self))
    def _():
        pl.semaphore_signal(barrier, inc=1, device_id=at(gx, gy, gz, gc), device_id_type=MESH)

    wide = a_ref[...].astype(F32)
    spread = jnp.sqrt(jnp.sum(wide * wide, axis=0, keepdims=True) * INV + 1e-06)
    e = jnp.full_like(spread, 2.0**10)
    for k in range(-9, 5):
        e = jnp.where(spread >= 2.0**k, 2.0**-k, e)
    se = spread * e
    factor = 1.0 / (se * se * se * e)
    scaled = wide * e
    jbuf[0, 0:256, :] = scaled.T.astype(BF16)
    jbuf[0, 256:320, :] = v_ref[:, 0:128]
    jbuf[0, 320:384, :] = v_ref[:, 128:256]
    line = lax.broadcasted_iota(jnp.int32, (16, 128), 0)
    rows = jnp.zeros((16, 128), F32)
    for half in range(2):
        for n, part in enumerate(split_three(factor[:, half * 128:half * 128 + 128])):
            rows = jnp.where(line == half * 8 + n, part, rows)
    rows = rows.astype(BF16)
    jbuf[0, 384:400, :] = rows
    narrow = scaled.astype(BF16)
    imsg[0:128, :] = narrow[:, 0:128]
    imsg[128:256, :] = narrow[:, 128:256]
    imsg[256:272, :] = rows

    n_targets = jnp.where(gives, 2, 0) - jnp.where(own_lo | own_hi, 1, 0)
    pl.semaphore_wait(barrier, 7 + n_targets)

    sent = []

    def send(src, dst, recv, dev):
        copy = pltpu.make_async_remote_copy(
            src_ref=src, dst_ref=dst, send_sem=send_sem.at[len(sent)], recv_sem=recv,
            device_id=dev, device_id_type=MESH,
        )
        sent.append(copy)
        copy.start()

    def arrived(dst, recv):
        pltpu.make_async_remote_copy(
            src_ref=dst, dst_ref=dst, send_sem=send_sem.at[0], recv_sem=recv,
            device_id=sib, device_id_type=MESH,
        ).wait_recv()

    def seed(n, is_self):
        return pltpu.make_async_remote_copy(
            src_ref=imsg, dst_ref=ibuf.at[sd], send_sem=local_sem.at[n], recv_sem=irecv.at[0],
            device_id=at(tx, ty, sd + 8 * n, tc), device_id_type=MESH,
        ), gives & jnp.logical_not(is_self)

    seeds = [seed(0, own_lo), seed(1, own_hi)]
    for copy, cond in seeds:
        pl.when(cond)(copy.start)

    def jsend(src, dst, dev):
        send(jbuf.at[src], jbuf.at[dst], jrecv.at[dst], dev)

    def jwait(n):
        arrived(jbuf.at[n], jrecv.at[n])

    def to_sib(n):
        jsend(n, 16 + n, sib)

    def prep(n):
        rows = jbuf[n, 384:400, :].astype(F32)
        for half in range(2):
            f = jnp.sum(rows[half * 8:half * 8 + 8, :], axis=0, keepdims=True)
            w = jbuf[n, 256 + half * 64:320 + half * 64, :].astype(F32) * f
            hi = w.astype(BF16)
            lo = (w - hi.astype(F32)).astype(BF16)
            lanes = slice(n * 256 + half * 128, n * 256 + half * 128 + 128)
            vbuf[0:64, lanes] = hi
            vbuf[64:128, lanes] = lo

    def q_both(dp, dq):
        n = SLOT[dp, dq]
        jsend(n, SLOT[dp, (dq + 3) % 4], q_up)
        jsend(n, SLOT[dp, (dq + 1) % 4], q_dn)

    def q_across(dp):
        f = (p + q + dp) % 2
        n1, n3 = SLOT[dp, 1], SLOT[dp, 3]
        src = n1 + f * (n3 - n1)
        jsend(src, SLOT[dp, 2], at_pq(p, (q + 3 + 2 * f) % 4))

    jsend(0, SLOT[3, 0], p_up)
    jsend(0, SLOT[1, 0], p_dn)
    q_both(0, 0)
    to_sib(0)
    prep(0)

    def ichunk(s):
        return ibuf.at[s]

    def isend(k, dev, step):
        s = (z + k + 8) % 8
        send(ichunk(s), ichunk(s), irecv.at[step], dev)

    def iwait(k, step):
        s = (z + k + 8) % 8
        arrived(ichunk(s), irecv.at[step])

    def tile(groups, weights):
        total = None
        for first, n in groups:
            states = jbuf[first:first + n, 0:256, :].reshape(n * 256, 128)
            prod = dot(states, weights)
            square = prod * prod
            local = (square * square).astype(BF16)
            part = dot(vbuf[:, first * 256:(first + n) * 256], local)
            total = part if total is None else total + part
        return total[0:64, :] + total[64:128, :]

    def early_tiles(ks):
        parts, rels = [], []
        for k in ks:
            s = (z + k + 8) % 8
            for half in range(2):
                parts.append(ibuf[s, half * 128:half * 128 + 128, :])
                rels.append((2 * s + half - z + 16) % 16)
        total = tile(EARLY, jnp.concatenate(parts, axis=1))
        for n, rel in enumerate(rels):
            acc[rel] = total[:, n * 128:n * 128 + 128]

    @pl.when(from_self)
    def _():
        copy = pltpu.make_async_copy(imsg, ibuf.at[s0], local_sem.at[2])
        copy.start()
        copy.wait()

    @pl.when(jnp.logical_not(from_self))
    def _():
        arrived(ibuf.at[s0], irecv.at[0])

    isend(0, z_up, 1)
    isend(0, z_dn, 5)

    jwait(SLOT[1, 0])
    jwait(SLOT[3, 0])
    f = p % 2
    jsend(SLOT[1, 0] + f * (SLOT[3, 0] - SLOT[1, 0]), SLOT[2, 0], at_pq((p + 3 + 2 * f) % 4, q))
    q_both(1, 0)
    q_both(3, 0)
    to_sib(SLOT[1, 0])
    to_sib(SLOT[3, 0])
    jwait(SLOT[0, 1])
    jwait(SLOT[0, 3])
    q_across(0)
    to_sib(SLOT[0, 1])
    to_sib(SLOT[0, 3])
    for n in range(1, 5):
        prep(n)
    for n in range(16, 21):
        jwait(n)
        prep(n)

    early_tiles([0])
    iwait(-1, 1)
    isend(-1, z_up, 2)
    iwait(1, 5)
    isend(1, z_dn, 6)
    jwait(SLOT[2, 0])
    q_both(2, 0)
    to_sib(SLOT[2, 0])
    jwait(SLOT[0, 2])
    to_sib(SLOT[0, 2])
    early_tiles([-1, 1])
    iwait(-2, 2)
    isend(-2, z_up, 3)
    iwait(2, 6)
    isend(2, z_dn, 7)
    for dp in (1, 3):
        jwait(SLOT[dp, 1])
        jwait(SLOT[dp, 3])
        q_across(dp)
        to_sib(SLOT[dp, 1])
        to_sib(SLOT[dp, 3])
    early_tiles([-2, 2])
    iwait(-3, 3)
    isend(-3, z_up, 4)
    iwait(3, 7)
    jwait(SLOT[2, 1])
    jwait(SLOT[2, 3])
    q_across(2)
    to_sib(SLOT[2, 1])
    to_sib(SLOT[2, 3])
    for dp in (1, 3):
        jwait(SLOT[dp, 2])
        to_sib(SLOT[dp, 2])
    early_tiles([-3, 3])
    iwait(-4, 4)
    jwait(SLOT[2, 2])
    to_sib(SLOT[2, 2])
    early_tiles([-4])
    for n in list(range(5, 16)):
        prep(n)
    for n in range(21, 32):
        jwait(n)
        prep(n)

    def chunk(rel):
        d = (z + rel) % 16
        return ibuf[d // 2, pl.ds(pl.multiple_of((d % 2) * 128, 128), 128), :]

    for k in range(8):
        below, above = 8 + k, (8 - k) % 8
        total = tile(LATE, jnp.concatenate([chunk(below), chunk(above)], axis=1))
        acc[below] += total[:, 0:128]
        acc[above] += total[:, 128:256]
        if k >= 1:
            arrived(rsm.at[k - 1], mrecv.at[k - 1])
            acc[below] += rsm[k - 1]
        send(acc.at[below], rsm.at[k], mrecv.at[k], z_dn)
        if k >= 2:
            arrived(rsp.at[k - 2], precv.at[k - 2])
            acc[above] += rsp[k - 2]
        if k >= 1:
            send(acc.at[above], rsp.at[k - 1], precv.at[k - 1], z_up)

    half = z % 2
    rows = ibuf[z // 2, 256:272, :].astype(F32)
    f0 = jnp.sum(rows[0:8, :], axis=0, keepdims=True)
    f1 = jnp.sum(rows[8:16, :], axis=0, keepdims=True)
    scale = jnp.where(half == 0, f0, f1) * (INV**4)
    arrived(rsm.at[7], mrecv.at[7])
    arrived(rsp.at[6], precv.at[6])
    o_ref[...] = (acc[0] + rsm[7] + rsp[6]) * scale

    for copy in sent:
        copy.wait_send()
    for copy, cond in seeds:
        pl.when(cond)(copy.wait_send)


def per_device(anomalies, vectors):
    vmem = pl.BlockSpec(memory_space=pltpu.VMEM)
    return pl.pallas_call(
        kernel,
        out_shape=jax.ShapeDtypeStruct((VECS, 128), F32),
        in_specs=[vmem, vmem],
        out_specs=vmem,
        scratch_shapes=[
            pltpu.VMEM((32, JROWS, 128), BF16),
            pltpu.VMEM((128, 8192), BF16),
            pltpu.VMEM((8, IROWS, 128), BF16),
            pltpu.VMEM((IROWS, 128), BF16),
            pltpu.VMEM((16, VECS, 128), F32),
            pltpu.VMEM((8, VECS, 128), F32),
            pltpu.VMEM((7, VECS, 128), F32),
            pltpu.SemaphoreType.DMA((80,)),
            pltpu.SemaphoreType.DMA((32,)),
            pltpu.SemaphoreType.DMA((8,)),
            pltpu.SemaphoreType.DMA((8,)),
            pltpu.SemaphoreType.DMA((7,)),
            pltpu.SemaphoreType.DMA((3,)),
        ],
        compiler_params=pltpu.CompilerParams(
            collective_id=0, has_side_effects=True, vmem_limit_bytes=48 * 2**20
        ),
    )(anomalies, vectors)


def solution(mesh):
    return jax.shard_map(
        per_device,
        mesh=mesh,
        in_specs=(P(None, ("col", "row")), P(None, ("col", "row"))),
        out_specs=P(None, ("row", "col")),
        check_vma=False,
    )
```

```python
import jax
import jax.numpy as jnp
from jax import lax
from jax.experimental import pallas as pl
from jax.experimental.pallas import tpu as pltpu
from jax.sharding import PartitionSpec as P

MESH = pl.DeviceIdType.MESH
F32 = jnp.float32
BF16 = jnp.bfloat16
MEMBERS = 128
VECS = 64
INV = 1.0 / (MEMBERS - 1.0)
JROWS = 400
IROWS = 144

ORDER = [
    (0, 0), (1, 0), (3, 0), (0, 1), (0, 3), (2, 0), (0, 2), (1, 1),
    (1, 3), (3, 1), (3, 3), (1, 2), (3, 2), (2, 1), (2, 3), (2, 2),
]
SLOT = {off: n for n, off in enumerate(ORDER)}
FIRST = [(0, 5), (16, 5)]
SECOND = [(5, 6), (21, 6)]
THIRD = [(11, 5), (27, 5)]


def dot(a, b):
    return jnp.dot(a, b, preferred_element_type=F32)


def split_three(c):
    hi = c.astype(BF16).astype(F32)
    rest = c - hi
    mid = rest.astype(BF16).astype(F32)
    return hi, mid, rest - mid


def kernel(a_ref, v_ref, o_ref, jbuf, vbuf, ibuf, imsg, acc, outbox, inbox,
           send_sem, jrecv, irecv, rrecv, misc, zsem, wsem, xsem, ysem, csem):
    row, col = lax.axis_index("row"), lax.axis_index("col")
    x, zh, core = row // 4, (row // 2) % 2, row % 2
    y, zl = col // 8, col % 8
    z = zh * 8 + zl

    def at(x_, y_, z_, core_):
        return {"row": x_ * 4 + (z_ // 8) * 2 + core_, "col": y_ * 8 + z_ % 8}

    p = x + core * (y - x)
    q = y + core * (x - y)

    def at_pq(dp, dq):
        p_, q_ = (p + dp) % 4, (q + dq) % 4
        return at(p_ + core * (q_ - p_), q_ + core * (p_ - q_), z, core)

    def at_z(d):
        return at(x, y, (z + d + 16) % 16, core)

    def signal(sem, dev):
        pl.semaphore_signal(sem, inc=1, device_id=dev, device_id_type=MESH)

    sib = at(x, y, z, 1 - core)
    mirror = at(x, 3 - y, z, core)
    half = y // 2
    source_y = y + half * (3 - 2 * y)

    barrier = pltpu.get_barrier_semaphore()
    partners = [sib] + [at_pq(d, 0) for d in (1, 2, 3)] + [at_pq(0, d) for d in (1, 2, 3)]
    partners += [at_z(d) for d in (1, -1, 2, -2, 3, -3)]
    for dev in partners:
        signal(barrier, dev)

    wide = a_ref[...].astype(F32)
    spread = jnp.sqrt(jnp.sum(wide * wide, axis=0, keepdims=True) * INV + 1e-06)
    e = jnp.full_like(spread, 2.0**10)
    for k in range(-9, 5):
        e = jnp.where(spread >= 2.0**k, 2.0**-k, e)
    se = spread * e
    factor = 1.0 / (se * se * se * e)
    scaled = wide * e
    narrow = scaled.astype(BF16)
    line = lax.broadcasted_iota(jnp.int32, (16, 128), 0)
    zero = jnp.zeros((16, 128), F32)
    halves = []
    for h in range(2):
        rows = zero
        for n, part in enumerate(split_three(factor[:, h * 128:h * 128 + 128])):
            rows = jnp.where(line == h * 8 + n, part, rows)
        halves.append(rows)

    @pl.when(y < 2)
    def _():
        ibuf[0, 0:128, :] = narrow[:, 0:128]
        ibuf[0, 128:144, :] = halves[0].astype(BF16)
        imsg[0:128, :] = narrow[:, 128:256]
        imsg[128:144, :] = halves[1].astype(BF16)

    jbuf[0, 0:256, :] = scaled.T.astype(BF16)
    jbuf[0, 256:320, :] = v_ref[:, 0:128]
    jbuf[0, 320:384, :] = v_ref[:, 128:256]
    jbuf[0, 384:400, :] = (halves[0] + halves[1]).astype(BF16)

    pl.semaphore_wait(barrier, len(partners))

    sent = []

    def remote(src, dst, recv, dev):
        copy = pltpu.make_async_remote_copy(
            src_ref=src, dst_ref=dst, send_sem=send_sem.at[len(sent)], recv_sem=recv,
            device_id=dev, device_id_type=MESH,
        )
        sent.append(copy)
        return copy

    def send(*args):
        remote(*args).start()

    def arrived(dst, recv):
        pltpu.make_async_remote_copy(
            src_ref=dst, dst_ref=dst, send_sem=misc.at[0], recv_sem=recv,
            device_id=sib, device_id_type=MESH,
        ).wait_recv()

    def isend(k, d):
        dst = (k - d) % 16
        send(ibuf.at[k % 16], ibuf.at[dst], irecv.at[dst], at_z(d))

    def iwait(*ks):
        for k in ks:
            arrived(ibuf.at[k % 16], irecv.at[k % 16])

    def jsend(src, dst, dev):
        send(jbuf.at[src], jbuf.at[dst], jrecv.at[dst], dev)

    def jwait(n):
        arrived(jbuf.at[n], jrecv.at[n])

    def to_sib(n):
        jsend(n, 16 + n, sib)

    def along_q(dp):
        for d in (1, 3, 2):
            jsend(SLOT[dp, 0], SLOT[dp, (4 - d) % 4], at_pq(0, d))

    def prep(n):
        rows = jbuf[n, 384:400, :].astype(F32)
        for h in range(2):
            f = jnp.sum(rows[h * 8:h * 8 + 8, :], axis=0, keepdims=True)
            w = jbuf[n, 256 + h * 64:320 + h * 64, :].astype(F32) * f
            hi = w.astype(BF16)
            lo = (w - hi.astype(F32)).astype(BF16)
            lanes = slice(n * 256 + h * 128, n * 256 + h * 128 + 128)
            vbuf[0:64, lanes] = hi
            vbuf[64:128, lanes] = lo

    hand_over = remote(imsg, ibuf.at[0], irecv.at[0], mirror)
    pl.when(y < 2)(hand_over.start)
    sent.pop()
    sent.append(None)
    for d in (1, 3, 2):
        jsend(0, SLOT[4 - d, 0], at_pq(d, 0))
    along_q(0)
    to_sib(0)
    for d in (3, -3):
        signal(zsem, at_z(d))

    @pl.when(y >= 2)
    def _():
        arrived(ibuf.at[0], irecv.at[0])

    for d in (3, -3, 1, -1, 2, -2):
        isend(0, d)
    prep(0)

    def tile(groups, chunks):
        weights = jnp.concatenate(chunks, axis=1)
        total = None
        for first, n in groups:
            states = jbuf[first:first + n, 0:256, :].reshape(n * 256, 128)
            prod = dot(states, weights)
            square = prod * prod
            local = (square * square).astype(BF16)
            part = dot(vbuf[:, first * 256:(first + n) * 256], local)
            total = part if total is None else total + part
        return total[0:64, :] + total[64:128, :]

    def add_tiles(groups, ks, fresh):
        total = tile(groups, [ibuf[k % 16, 0:128, :] for k in ks])
        for n, k in enumerate(ks):
            part = total[:, n * 128:n * 128 + 128]
            acc[k % 16] = part if fresh else acc[k % 16] + part

    for dp in (1, 3, 2):
        n = SLOT[dp, 0]
        jwait(n)
        along_q(dp)
        to_sib(n)
    for dq in (1, 3):
        n = SLOT[0, dq]
        jwait(n)
        to_sib(n)
    pl.semaphore_wait(zsem, 2)
    for d in (5, -5):
        signal(wsem, at_z(d))
    iwait(-3)
    for d in (3, 1, 2):
        isend(-3, d)
    iwait(3)
    for d in (-3, -1, -2):
        isend(3, d)
    for n in range(16, 21):
        jwait(n)
    iwait(-1, 1, -2, 2)
    for n in list(range(1, 5)) + list(range(16, 21)):
        prep(n)
    wave = [1, -1, 2, -2, 3, -3]
    add_tiles(FIRST, wave, True)

    pl.semaphore_wait(wsem, 2)
    for d in (1, 2, 3):
        signal(xsem, at((x + d) % 4, y, z, core))
    for off in ORDER[6:11]:
        jwait(SLOT[off])
        to_sib(SLOT[off])
    for n in range(21, 27):
        jwait(n)
    for n in list(range(5, 11)) + list(range(21, 27)):
        prep(n)
    add_tiles(SECOND, wave, False)

    pl.semaphore_wait(xsem, 3)
    for d in (1, 2, 3):
        signal(ysem, at(x, (y + d) % 4, z, core))
    iwait(-6)
    isend(-6, 1)
    isend(-6, 2)
    iwait(6)
    isend(6, -1)
    iwait(-4, 4, -5, 5)
    for off in ORDER[11:]:
        jwait(SLOT[off])
        to_sib(SLOT[off])
    add_tiles(FIRST + SECOND, [4, -4, 5, -5, 6, -6], True)

    pl.semaphore_wait(ysem, 3)
    signal(csem, sib)
    iwait(7, -7, 8)
    for n in range(27, 32):
        jwait(n)
    for n in list(range(11, 16)) + list(range(27, 32)):
        prep(n)
    add_tiles(FIRST + SECOND, [0, 7, -7, 8], True)
    pl.semaphore_wait(csem, 1)

    near = ((z - 2 * core - half + 2 + 16) // 4) % 4
    outs = []
    for step, turn in enumerate((2, 1, 3, 0)):
        g = (near + turn) % 4
        h, zs_hi = g // 2, g % 2
        rels = [(8 * zs_hi + 4 * a + 2 * h + b - z + 16) % 16 for a in range(2) for b in range(2)]
        total = tile(THIRD, [ibuf[rel, 0:128, :] for rel in rels])
        for n, rel in enumerate(rels):
            rows = ibuf[rel, 128:144, :].astype(F32)
            scale = jnp.sum(rows, axis=0, keepdims=True) * (INV**4)
            part = acc[rel] + total[:, n * 128:n * 128 + 128]
            m = 4 * step + n
            outbox[m] = (part * scale).astype(BF16)
            dx, dy, dz, dc = 2 * source_y + n // 2, x, 8 * h + 4 * zs_hi + 2 * core + half, n % 2
            mine = (dx == x) & (dy == y) & (dz == z) & (dc == core)
            copy = remote(outbox.at[m], inbox.at[z], rrecv.at[z], at(dx, dy, dz, dc))
            sent.pop()
            sent.append(None)
            pl.when(jnp.logical_not(mine))(copy.start)
            stay = pltpu.make_async_copy(outbox.at[m], inbox.at[z], rrecv.at[z])
            pl.when(mine)(stay.start)
            outs.append((copy, jnp.logical_not(mine)))

    result = None
    for n in range(16):
        arrived(inbox.at[n], rrecv.at[n])
    for n in range(16):
        part = inbox[n].astype(F32)
        result = part if result is None else result + part
    o_ref[...] = result

    for copy in sent:
        if copy is not None:
            copy.wait_send()
    pl.when(y < 2)(hand_over.wait_send)
    for copy, cond in outs:
        pl.when(cond)(copy.wait_send)


def per_device(anomalies, vectors):
    vmem = pl.BlockSpec(memory_space=pltpu.VMEM)
    return pl.pallas_call(
        kernel,
        out_shape=jax.ShapeDtypeStruct((VECS, 128), F32),
        in_specs=[vmem, vmem],
        out_specs=vmem,
        scratch_shapes=[
            pltpu.VMEM((32, JROWS, 128), BF16),
            pltpu.VMEM((128, 8192), BF16),
            pltpu.VMEM((16, IROWS, 128), BF16),
            pltpu.VMEM((IROWS, 128), BF16),
            pltpu.VMEM((16, VECS, 128), F32),
            pltpu.VMEM((16, VECS, 128), BF16),
            pltpu.VMEM((16, VECS, 128), BF16),
            pltpu.SemaphoreType.DMA((64,)),
            pltpu.SemaphoreType.DMA((32,)),
            pltpu.SemaphoreType.DMA((16,)),
            pltpu.SemaphoreType.DMA((16,)),
            pltpu.SemaphoreType.DMA((1,)),
        ] + [pltpu.SemaphoreType.REGULAR] * 5,
        compiler_params=pltpu.CompilerParams(
            collective_id=0, has_side_effects=True, vmem_limit_bytes=48 * 2**20
        ),
    )(anomalies, vectors)


def solution(mesh):
    return jax.shard_map(
        per_device,
        mesh=mesh,
        in_specs=(P(None, ("col", "row")), P(None, ("col", "row"))),
        out_specs=P(None, ("row", "col")),
        check_vma=False,
    )
```

```python
import jax
import jax.numpy as jnp
from jax import lax
from jax.experimental import pallas as pl
from jax.experimental.pallas import tpu as pltpu
from jax.sharding import PartitionSpec as P

MESH = pl.DeviceIdType.MESH
F32 = jnp.float32
BF16 = jnp.bfloat16
MEMBERS = 128
VECS = 64
INV = 1.0 / (MEMBERS - 1.0)
JROWS = 400
IROWS = 144
NEAR_Z = (3, -3, 1, -1, 2, -2)

ORDER = [
    (0, 0), (1, 0), (3, 0), (0, 1), (0, 3), (2, 0), (0, 2), (1, 1),
    (1, 3), (3, 1), (3, 3), (1, 2), (3, 2), (2, 1), (2, 3), (2, 2),
]
SLOT = {off: n for n, off in enumerate(ORDER)}
FIRST = [(0, 5), (16, 5)]
REST = [(5, 6), (11, 5), (21, 6), (27, 5)]
TURNS = ((2, 1, 3, 0), (0, 3, 2, 1), (0, 1, 3, 2), (0, 1, 2, 3))


def dot(a, b):
    return jnp.dot(a, b, preferred_element_type=F32)


def split_three(c):
    hi = c.astype(BF16).astype(F32)
    rest = c - hi
    mid = rest.astype(BF16).astype(F32)
    return hi, mid, rest - mid


def kernel(a_hbm, v_hbm, o_ref, a_ref, v_ref, jbuf, vbuf, ibuf, imsg, fto, acc, outbox, inbox,
           send_sem, jrecv, irecv, rrecv, misc, zsem, wsem, xsem, csem):
    loads = [pltpu.make_async_copy(a_hbm, a_ref, misc.at[1]), pltpu.make_async_copy(v_hbm, v_ref, misc.at[2])]
    for copy in loads:
        copy.start()
    row, col = lax.axis_index("row"), lax.axis_index("col")
    x, zh, core = row // 4, (row // 2) % 2, row % 2
    y, zl = col // 8, col % 8
    z = zh * 8 + zl

    def at(x_, y_, z_, core_):
        return {"row": x_ * 4 + (z_ // 8) * 2 + core_, "col": y_ * 8 + z_ % 8}

    p = x + core * (y - x)
    q = y + core * (x - y)

    def at_pq(dp, dq):
        p_, q_ = (p + dp) % 4, (q + dq) % 4
        return at(p_ + core * (q_ - p_), q_ + core * (p_ - q_), z, core)

    def at_z(d, y_=y):
        return at(x, y_, (z + d + 16) % 16, core)

    def signal(sem, dev):
        pl.semaphore_signal(sem, inc=1, device_id=dev, device_id_type=MESH)

    sib = at(x, y, z, 1 - core)

    def same(x_, y_):
        return (x == x_) & (y == y_)

    gives = [(y < 2) & jnp.logical_not(same(2 * y + n, x)) for n in range(2)]
    keeps = [(y < 2) & same(2 * y + n, x) for n in range(2)]
    gets = jnp.logical_not(same(y, x // 2))

    barrier = pltpu.get_barrier_semaphore()
    partners = [sib] + [at_pq(d, 0) for d in (1, 2, 3)] + [at_pq(0, d) for d in (1, 2, 3)]
    partners += [at_z(d) for d in NEAR_Z]
    for dev in partners:
        signal(barrier, dev)

    @pl.when(gets)
    def _():
        signal(barrier, at(y, x // 2, z, core))

    for copy in loads:
        copy.wait()

    wide = a_ref[...].astype(F32)
    spread = jnp.sqrt(jnp.sum(wide * wide, axis=0, keepdims=True) * INV + 1e-06)
    e = jnp.full_like(spread, 2.0**10)
    for k in range(-9, 5):
        e = jnp.where(spread >= 2.0**k, 2.0**-k, e)
    se = spread * e
    factor = 1.0 / (se * se * se * e)
    scaled = wide * e
    narrow = scaled.astype(BF16)
    line = lax.broadcasted_iota(jnp.int32, (16, 128), 0)
    zero = jnp.zeros((16, 128), F32)
    halves = []
    for h in range(2):
        rows = zero
        for n, part in enumerate(split_three(factor[:, h * 128:h * 128 + 128])):
            rows = jnp.where(line == h * 8 + n, part, rows)
        halves.append(rows)

    for n in range(2):
        imsg[n, 0:128] = narrow[:, n * 128:n * 128 + 128]
        imsg[n, 128:144] = halves[n].astype(BF16)

        @pl.when(keeps[n])
        def _():
            ibuf[0] = imsg[n]


    jbuf[0, 0:256, :] = scaled.T.astype(BF16)
    jbuf[0, 256:320, :] = v_ref[:, 0:128]
    jbuf[0, 320:384, :] = v_ref[:, 128:256]
    jbuf[0, 384:400, :] = (halves[0] + halves[1]).astype(BF16)

    pl.semaphore_wait(barrier, len(partners) + sum(g.astype(jnp.int32) for g in gives))

    sent = []

    def remote(src, dst, recv, dev):
        copy = pltpu.make_async_remote_copy(
            src_ref=src, dst_ref=dst, send_sem=send_sem.at[len(sent)], recv_sem=recv,
            device_id=dev, device_id_type=MESH,
        )
        sent.append(copy)
        return copy

    def send(*args):
        remote(*args).start()

    def arrived(dst, recv):
        pltpu.make_async_remote_copy(
            src_ref=dst, dst_ref=dst, send_sem=misc.at[0], recv_sem=recv,
            device_id=sib, device_id_type=MESH,
        ).wait_recv()

    def ichunk(slot):
        return ibuf.at[slot, 0:128]

    def isend(k, d):
        dst = (k - d) % 16
        send(ichunk(k % 16), ichunk(dst), irecv.at[dst], at_z(d))

    def iwait(*ks):
        for k in ks:
            arrived(ichunk(k % 16), irecv.at[k % 16])

    started = []

    def send_if(cond, *args):
        copy = remote(*args)
        sent[-1] = None
        pl.when(cond)(copy.start)
        started.append((copy, cond))

    def jsend(src, dst, dev):
        send(jbuf.at[src], jbuf.at[dst], jrecv.at[dst], dev)

    def jwait(n):
        arrived(jbuf.at[n], jrecv.at[n])

    def to_sib(n):
        jsend(n, 16 + n, sib)

    def along_q(dp):
        for d in (1, 3) if dp % 2 else (1, 3, 2):
            jsend(SLOT[dp, 0], SLOT[dp, 4 - d], at_pq(0, d))

    def across_q(dp):
        jsend(SLOT[dp, 1], SLOT[dp, 2], at_pq(0, 3))

    def prep(n):
        rows = jbuf[n, 384:400, :].astype(F32)
        for h in range(2):
            f = jnp.sum(rows[h * 8:h * 8 + 8, :], axis=0, keepdims=True)
            w = jbuf[n, 256 + h * 64:320 + h * 64, :].astype(F32) * f
            hi = w.astype(BF16)
            lo = (w - hi.astype(F32)).astype(BF16)
            lanes = slice(n * 256 + h * 128, n * 256 + h * 128 + 128)
            vbuf[0:64, lanes] = hi
            vbuf[64:128, lanes] = lo

    for n in range(2):
        send_if(gives[n], imsg.at[n], ibuf.at[0], irecv.at[0], at((2 * y + n) % 4, x, z, core))
    for d in (1, 3, 2):
        jsend(0, SLOT[4 - d, 0], at_pq(d, 0))
    along_q(0)
    to_sib(0)

    @pl.when(gets)
    def _():
        arrived(ibuf.at[0], irecv.at[0])

    for d in NEAR_Z:
        isend(0, d)
    for d in (3, -3):
        signal(zsem, at_z(d))
    prep(0)

    def tile(groups, chunks):
        weights = jnp.concatenate(chunks, axis=1)
        total = None
        for first, n in groups:
            states = jbuf[first:first + n, 0:256, :].reshape(n * 256, 128)
            prod = dot(states, weights)
            square = prod * prod
            local = (square * square).astype(BF16)
            part = dot(vbuf[:, first * 256:(first + n) * 256], local)
            total = part if total is None else total + part
        return total[0:64, :] + total[64:128, :]

    def add_tiles(groups, ks, fresh):
        total = tile(groups, [ibuf[k % 16, 0:128] for k in ks])
        for n, k in enumerate(ks):
            part = total[:, n * 128:n * 128 + 128]
            acc[k % 16] = part if fresh else acc[k % 16] + part

    def take(*offs):
        for off in offs:
            jwait(SLOT[off])
            to_sib(SLOT[off])

    for dp in (1, 3):
        take((dp, 0))
        along_q(dp)
    take((0, 1), (0, 3))
    take((2, 0))
    along_q(2)
    pl.semaphore_wait(zsem, 2)
    for d in (5, -5):
        signal(wsem, at_z(d))
    iwait(-3)
    for d in (3, 1, 2):
        isend(-3, d)
    iwait(3)
    for d in (-3, -1, -2):
        isend(3, d)
    for n in range(1, 5):
        prep(n)
    for n in range(16, 21):
        jwait(n)
        prep(n)
    iwait(-1, 1, -2, 2)
    add_tiles(FIRST, [1, -1, 2, -2, 3, -3], True)

    pl.semaphore_wait(wsem, 2)
    signal(xsem, at(x + 1 - 2 * (x % 2), y, z, core))
    for dp in (1, 3):
        take((dp, 1), (dp, 3))
        across_q(dp)
    take((0, 2))
    for n in range(5, 11):
        prep(n)
    iwait(-6)
    isend(-6, 1)
    isend(-6, 2)
    iwait(6)
    isend(6, -1)
    pl.semaphore_wait(xsem, 1)
    signal(csem, sib)
    for n in range(21, 27):
        jwait(n)
        prep(n)
    iwait(-4, 4, -5, 5)
    add_tiles(FIRST, [4, -4, 5, -5, 6, -6], True)
    take((2, 1), (2, 3))
    take((1, 2), (3, 2), (2, 2))
    for n in range(11, 16):
        prep(n)
    for n in range(27, 32):
        jwait(n)
        prep(n)
    pl.semaphore_wait(csem, 1)

    def deliver(src, dst, recv, zs):
        bit, h = x % 2, (zs // 2) % 2
        dx, dz, dc = x - bit + (zs // 4) % 2, 8 * h + 4 * (zs // 8) + 2 * core + bit, zs % 2
        mine = (dx == x) & (dz == z) & (dc == core)
        send_if(jnp.logical_not(mine), src, dst, recv, at(dx, y, dz, dc))
        pl.when(mine)(pltpu.make_async_copy(src, dst, recv).start)

    deliver(ibuf.at[0, 128:144], fto, misc.at[3], z)

    iwait(7, -7, 8)
    add_tiles(FIRST, [0, 7, -7, 8], True)
    near = ((z - 2 * core - x % 2 + 18) // 4) % 4
    for step in range(4):
        g = sum((near == n).astype(jnp.int32) * turn[step] for n, turn in enumerate(TURNS))
        h, zs_hi = g // 2, g % 2
        begins = [8 * zs_hi + 4 * a + 2 * h + b for a in range(2) for b in range(2)]
        rels = [(zs - z + 16) % 16 for zs in begins]
        total = tile(REST, [ibuf[rel, 0:128] for rel in rels])
        for n, rel in enumerate(rels):
            outbox[4 * step + n] = (acc[rel] + total[:, n * 128:n * 128 + 128]).astype(BF16)
        for n in range(4):
            deliver(outbox.at[4 * step + n], inbox.at[z], rrecv.at[z], begins[n])

    result = None
    arrived(fto, misc.at[3])
    for n in range(16):
        arrived(inbox.at[n], rrecv.at[n])
    for n in range(16):
        part = inbox[n].astype(F32)
        result = part if result is None else result + part
    o_ref[...] = result * (jnp.sum(fto[...].astype(F32), axis=0, keepdims=True) * INV**4)

    for copy in sent:
        if copy is not None:
            copy.wait_send()
    for copy, cond in started:
        pl.when(cond)(copy.wait_send)


def per_device(anomalies, vectors):
    vmem, hbm = pl.BlockSpec(memory_space=pltpu.VMEM), pl.BlockSpec(memory_space=pl.ANY)
    return pl.pallas_call(
        kernel,
        out_shape=jax.ShapeDtypeStruct((VECS, 128), F32),
        in_specs=[hbm, hbm],
        out_specs=vmem,
        scratch_shapes=[
            pltpu.VMEM((MEMBERS, 256), BF16),
            pltpu.VMEM((VECS, 256), BF16),
            pltpu.VMEM((32, JROWS, 128), BF16),
            pltpu.VMEM((128, 8192), BF16),
            pltpu.VMEM((16, IROWS, 128), BF16),
            pltpu.VMEM((2, IROWS, 128), BF16),
            pltpu.VMEM((16, 128), BF16),
            pltpu.VMEM((16, VECS, 128), F32),
            pltpu.VMEM((16, VECS, 128), BF16),
            pltpu.VMEM((16, VECS, 128), BF16),
            pltpu.SemaphoreType.DMA((80,)),
            pltpu.SemaphoreType.DMA((32,)),
            pltpu.SemaphoreType.DMA((16,)),
            pltpu.SemaphoreType.DMA((16,)),
            pltpu.SemaphoreType.DMA((4,)),
        ] + [pltpu.SemaphoreType.REGULAR] * 4,
        compiler_params=pltpu.CompilerParams(
            collective_id=0, has_side_effects=True, vmem_limit_bytes=48 * 2**20
        ),
    )(anomalies, vectors)


def solution(mesh):
    return jax.shard_map(
        per_device,
        mesh=mesh,
        in_specs=(P(None, ("col", "row")), P(None, ("col", "row"))),
        out_specs=P(None, ("row", "col")),
        check_vma=False,
    )
```

```python
import jax
import jax.numpy as jnp
from jax import lax
from jax.experimental import pallas as pl
from jax.experimental.pallas import tpu as pltpu
from jax.sharding import PartitionSpec as P

MESH = pl.DeviceIdType.MESH
F32 = jnp.float32
BF16 = jnp.bfloat16
MEMBERS = 128
VECS = 64
INV = 1.0 / (MEMBERS - 1.0)
JROWS = 400
IROWS = 144
NEAR_Z = (3, -3, 1, -1, 2, -2)

ORDER = [
    (0, 0), (1, 0), (3, 0), (0, 1), (0, 3), (2, 0), (0, 2), (1, 1),
    (1, 3), (3, 1), (3, 3), (1, 2), (3, 2), (2, 1), (2, 3), (2, 2),
]
SLOT = {off: n for n, off in enumerate(ORDER)}
FIRST = [(0, 5), (16, 5)]
REST = [(5, 6), (11, 5), (21, 6), (27, 5)]
TURNS = ((2, 1, 3, 0), (0, 3, 2, 1), (0, 1, 3, 2), (0, 1, 2, 3))


def dot(a, b):
    return jnp.dot(a, b, preferred_element_type=F32)


def split_three(c):
    hi = c.astype(BF16).astype(F32)
    rest = c - hi
    mid = rest.astype(BF16).astype(F32)
    return hi, mid, rest - mid


def kernel(a_hbm, v_hbm, o_ref, a_ref, v_ref, jbuf, vbuf, ibuf, imsg, fto, acc, outbox, inbox,
           send_sem, jrecv, irecv, rrecv, misc, zsem, wsem, xsem, csem):
    loads = [pltpu.make_async_copy(a_hbm, a_ref, misc.at[1]), pltpu.make_async_copy(v_hbm, v_ref, misc.at[2])]
    for copy in loads:
        copy.start()
    row, col = lax.axis_index("row"), lax.axis_index("col")
    x, zh, core = row // 4, (row // 2) % 2, row % 2
    y, zl = col // 8, col % 8
    z = zh * 8 + zl

    def at(x_, y_, z_, core_):
        return {"row": x_ * 4 + (z_ // 8) * 2 + core_, "col": y_ * 8 + z_ % 8}

    p = x + core * (y - x)
    q = y + core * (x - y)

    def at_pq(dp, dq):
        p_, q_ = (p + dp) % 4, (q + dq) % 4
        return at(p_ + core * (q_ - p_), q_ + core * (p_ - q_), z, core)

    def at_z(d, y_=y):
        return at(x, y_, (z + d + 16) % 16, core)

    def signal(sem, dev):
        pl.semaphore_signal(sem, inc=1, device_id=dev, device_id_type=MESH)

    sib = at(x, y, z, 1 - core)

    def same(x_, y_):
        return (x == x_) & (y == y_)

    gives = [(y < 2) & jnp.logical_not(same(2 * y + n, x)) for n in range(2)]
    keeps = [(y < 2) & same(2 * y + n, x) for n in range(2)]
    gets = jnp.logical_not(same(y, x // 2))

    barrier = pltpu.get_barrier_semaphore()
    partners = [sib] + [at_pq(d, 0) for d in (1, 2, 3)] + [at_pq(0, d) for d in (1, 2, 3)]
    partners += [at_z(d) for d in NEAR_Z]
    for dev in partners:
        signal(barrier, dev)

    @pl.when(gets)
    def _():
        signal(barrier, at(y, x // 2, z, core))

    for copy in loads:
        copy.wait()

    wide = a_ref[...].astype(F32)
    spread = jnp.sqrt(jnp.sum(wide * wide, axis=0, keepdims=True) * INV + 1e-06)
    e = jnp.full_like(spread, 2.0**10)
    for k in range(-9, 5):
        e = jnp.where(spread >= 2.0**k, 2.0**-k, e)
    se = spread * e
    factor = 1.0 / (se * se * se * e)
    scaled = wide * e
    narrow = scaled.astype(BF16)
    line = lax.broadcasted_iota(jnp.int32, (16, 128), 0)
    zero = jnp.zeros((16, 128), F32)
    halves = []
    for h in range(2):
        rows = zero
        for n, part in enumerate(split_three(factor[:, h * 128:h * 128 + 128])):
            rows = jnp.where(line == h * 8 + n, part, rows)
        halves.append(rows)

    for n in range(2):
        imsg[n, 0:128] = narrow[:, n * 128:n * 128 + 128]
        imsg[n, 128:144] = halves[n].astype(BF16)

        @pl.when(keeps[n])
        def _():
            ibuf[0] = imsg[n]


    jbuf[0, 0:256, :] = scaled.T.astype(BF16)
    jbuf[0, 256:320, :] = v_ref[:, 0:128]
    jbuf[0, 320:384, :] = v_ref[:, 128:256]
    jbuf[0, 384:400, :] = (halves[0] + halves[1]).astype(BF16)

    pl.semaphore_wait(barrier, len(partners) + sum(g.astype(jnp.int32) for g in gives))

    sent = []

    def remote(src, dst, recv, dev):
        copy = pltpu.make_async_remote_copy(
            src_ref=src, dst_ref=dst, send_sem=send_sem.at[len(sent)], recv_sem=recv,
            device_id=dev, device_id_type=MESH,
        )
        sent.append(copy)
        return copy

    def send(*args):
        remote(*args).start()

    def arrived(dst, recv):
        pltpu.make_async_remote_copy(
            src_ref=dst, dst_ref=dst, send_sem=misc.at[0], recv_sem=recv,
            device_id=sib, device_id_type=MESH,
        ).wait_recv()

    def ichunk(slot):
        return ibuf.at[slot, 0:128]

    def isend(k, d):
        dst = (k - d) % 16
        send(ichunk(k % 16), ichunk(dst), irecv.at[dst], at_z(d))

    def iwait(*ks):
        for k in ks:
            arrived(ichunk(k % 16), irecv.at[k % 16])

    started = []

    def send_if(cond, *args):
        copy = remote(*args)
        sent[-1] = None
        pl.when(cond)(copy.start)
        started.append((copy, cond))

    def jsend(src, dst, dev):
        send(jbuf.at[src], jbuf.at[dst], jrecv.at[dst], dev)

    def jwait(n):
        arrived(jbuf.at[n], jrecv.at[n])

    def to_sib(n):
        jsend(n, 16 + n, sib)

    def along_q(dp):
        for d in (1, 3) if dp % 2 else (1, 3, 2):
            jsend(SLOT[dp, 0], SLOT[dp, 4 - d], at_pq(0, d))

    def across_q(dp):
        jsend(SLOT[dp, 1], SLOT[dp, 2], at_pq(0, 3))

    def prep(n):
        rows = jbuf[n, 384:400, :].astype(F32)
        for h in range(2):
            f = jnp.sum(rows[h * 8:h * 8 + 8, :], axis=0, keepdims=True)
            w = jbuf[n, 256 + h * 64:320 + h * 64, :].astype(F32) * f
            hi = w.astype(BF16)
            lo = (w - hi.astype(F32)).astype(BF16)
            lanes = slice(n * 256 + h * 128, n * 256 + h * 128 + 128)
            vbuf[0:64, lanes] = hi
            vbuf[64:128, lanes] = lo

    for n in range(2):
        send_if(gives[n], imsg.at[n], ibuf.at[0], irecv.at[0], at((2 * y + n) % 4, x, z, core))
    for d in (1, 3, 2):
        jsend(0, SLOT[4 - d, 0], at_pq(d, 0))
    along_q(0)
    to_sib(0)

    @pl.when(gets)
    def _():
        arrived(ibuf.at[0], irecv.at[0])

    for d in NEAR_Z:
        isend(0, d)
    for d in (3, -3):
        signal(zsem, at_z(d))
    prep(0)

    def tile(groups, chunks):
        weights = jnp.concatenate(chunks, axis=1)
        total = None
        for first, n in groups:
            states = jbuf[first:first + n, 0:256, :].reshape(n * 256, 128)
            prod = dot(states, weights)
            square = prod * prod
            local = (square * square).astype(BF16)
            part = dot(vbuf[:, first * 256:(first + n) * 256], local)
            total = part if total is None else total + part
        return total[0:64, :] + total[64:128, :]

    def add_tiles(groups, ks, fresh):
        total = tile(groups, [ibuf[k % 16, 0:128] for k in ks])
        for n, k in enumerate(ks):
            part = total[:, n * 128:n * 128 + 128]
            acc[k % 16] = part if fresh else acc[k % 16] + part

    def take(*offs):
        for off in offs:
            jwait(SLOT[off])
            to_sib(SLOT[off])

    for dp in (1, 3):
        take((dp, 0))
        along_q(dp)
    take((0, 1), (0, 3))
    take((2, 0))
    along_q(2)
    pl.semaphore_wait(zsem, 2)
    for d in (5, -5):
        signal(wsem, at_z(d))
    iwait(-3)
    for d in (3, 1, 2):
        isend(-3, d)
    iwait(3)
    for d in (-3, -1, -2):
        isend(3, d)
    for n in range(1, 5):
        prep(n)
    for n in range(16, 21):
        jwait(n)
        prep(n)
    for dp in (1, 3):
        take((dp, 1), (dp, 3))
        across_q(dp)
    iwait(-1, 1, -2, 2)
    add_tiles(FIRST, [1, -1, 2, -2, 3, -3], True)
    take((0, 2))

    pl.semaphore_wait(wsem, 2)
    signal(xsem, at(x + 1 - 2 * (x % 2), y, z, core))
    for n in range(5, 11):
        prep(n)
    iwait(-6)
    isend(-6, 1)
    isend(-6, 2)
    iwait(6)
    isend(6, -1)
    pl.semaphore_wait(xsem, 1)
    signal(csem, sib)
    for n in range(21, 27):
        jwait(n)
        prep(n)
    take((2, 1), (2, 3))
    take((1, 2), (3, 2), (2, 2))
    iwait(-4, 4, -5, 5)
    add_tiles(FIRST, [4, -4, 5, -5, 6, -6], True)
    for n in range(11, 16):
        prep(n)
    for n in range(27, 32):
        jwait(n)
        prep(n)
    pl.semaphore_wait(csem, 1)

    def deliver(src, dst, recv, zs):
        bit, h = x % 2, (zs // 2) % 2
        dx, dz, dc = x - bit + (zs // 4) % 2, 8 * h + 4 * (zs // 8) + 2 * core + bit, zs % 2
        mine = (dx == x) & (dz == z) & (dc == core)
        send_if(jnp.logical_not(mine), src, dst, recv, at(dx, y, dz, dc))
        pl.when(mine)(pltpu.make_async_copy(src, dst, recv).start)

    deliver(ibuf.at[0, 128:144], fto, misc.at[3], z)

    iwait(7, -7, 8)
    add_tiles(FIRST, [0, 7, -7, 8], True)
    near = ((z - 2 * core - x % 2 + 18) // 4) % 4
    for step in range(4):
        g = sum((near == n).astype(jnp.int32) * turn[step] for n, turn in enumerate(TURNS))
        h, zs_hi = g // 2, g % 2
        begins = [8 * zs_hi + 4 * a + 2 * h + b for a in range(2) for b in range(2)]
        rels = [(zs - z + 16) % 16 for zs in begins]
        total = tile(REST, [ibuf[rel, 0:128] for rel in rels])
        for n, rel in enumerate(rels):
            outbox[4 * step + n] = (acc[rel] + total[:, n * 128:n * 128 + 128]).astype(BF16)
        for n in range(4):
            deliver(outbox.at[4 * step + n], inbox.at[z], rrecv.at[z], begins[n])

    result = None
    arrived(fto, misc.at[3])
    for n in range(16):
        arrived(inbox.at[n], rrecv.at[n])
    for n in range(16):
        part = inbox[n].astype(F32)
        result = part if result is None else result + part
    o_ref[...] = result * (jnp.sum(fto[...].astype(F32), axis=0, keepdims=True) * INV**4)

    for copy in sent:
        if copy is not None:
            copy.wait_send()
    for copy, cond in started:
        pl.when(cond)(copy.wait_send)


def per_device(anomalies, vectors):
    vmem, hbm = pl.BlockSpec(memory_space=pltpu.VMEM), pl.BlockSpec(memory_space=pl.ANY)
    return pl.pallas_call(
        kernel,
        out_shape=jax.ShapeDtypeStruct((VECS, 128), F32),
        in_specs=[hbm, hbm],
        out_specs=vmem,
        scratch_shapes=[
            pltpu.VMEM((MEMBERS, 256), BF16),
            pltpu.VMEM((VECS, 256), BF16),
            pltpu.VMEM((32, JROWS, 128), BF16),
            pltpu.VMEM((128, 8192), BF16),
            pltpu.VMEM((16, IROWS, 128), BF16),
            pltpu.VMEM((2, IROWS, 128), BF16),
            pltpu.VMEM((16, 128), BF16),
            pltpu.VMEM((16, VECS, 128), F32),
            pltpu.VMEM((16, VECS, 128), BF16),
            pltpu.VMEM((16, VECS, 128), BF16),
            pltpu.SemaphoreType.DMA((80,)),
            pltpu.SemaphoreType.DMA((32,)),
            pltpu.SemaphoreType.DMA((16,)),
            pltpu.SemaphoreType.DMA((16,)),
            pltpu.SemaphoreType.DMA((4,)),
        ] + [pltpu.SemaphoreType.REGULAR] * 4,
        compiler_params=pltpu.CompilerParams(
            collective_id=0, has_side_effects=True, vmem_limit_bytes=48 * 2**20
        ),
    )(anomalies, vectors)


def solution(mesh):
    return jax.shard_map(
        per_device,
        mesh=mesh,
        in_specs=(P(None, ("col", "row")), P(None, ("col", "row"))),
        out_specs=P(None, ("row", "col")),
        check_vma=False,
    )
```

```python
import jax
import jax.numpy as jnp
from jax import lax
from jax.experimental import pallas as pl
from jax.experimental.pallas import tpu as pltpu
from jax.sharding import PartitionSpec as P

MESH = pl.DeviceIdType.MESH
F32 = jnp.float32
BF16 = jnp.bfloat16
MEMBERS = 128
VECS = 64
INV = 1.0 / (MEMBERS - 1.0)
JROWS = 400
IROWS = 144
NEAR_Z = (3, -3, 1, -1, 2, -2)

ORDER = [
    (0, 0), (1, 0), (3, 0), (0, 1), (0, 3), (2, 0), (0, 2), (1, 1),
    (1, 3), (3, 1), (3, 3), (1, 2), (3, 2), (2, 1), (2, 3), (2, 2),
]
SLOT = {off: n for n, off in enumerate(ORDER)}
FIRST = [(0, 5), (16, 5)]
REST = [(5, 6), (11, 5), (21, 6), (27, 5)]
TURNS = ((2, 1, 3, 0), (0, 3, 2, 1), (0, 1, 3, 2), (0, 1, 2, 3))


def dot(a, b):
    return jnp.dot(a, b, preferred_element_type=F32)


def split_three(c):
    hi = c.astype(BF16).astype(F32)
    rest = c - hi
    mid = rest.astype(BF16).astype(F32)
    return hi, mid, rest - mid


def kernel(a_hbm, v_hbm, o_ref, a_ref, v_ref, jbuf, vbuf, ibuf, imsg, fto, acc, outbox, inbox,
           send_sem, jrecv, irecv, rrecv, misc, zsem, wsem, xsem, csem):
    loads = [pltpu.make_async_copy(a_hbm, a_ref, misc.at[1]), pltpu.make_async_copy(v_hbm, v_ref, misc.at[2])]
    for copy in loads:
        copy.start()
    row, col = lax.axis_index("row"), lax.axis_index("col")
    x, zh, core = row // 4, (row // 2) % 2, row % 2
    y, zl = col // 8, col % 8
    z = zh * 8 + zl

    def at(x_, y_, z_, core_):
        return {"row": x_ * 4 + (z_ // 8) * 2 + core_, "col": y_ * 8 + z_ % 8}

    p = x + core * (y - x)
    q = y + core * (x - y)

    def at_pq(dp, dq):
        p_, q_ = (p + dp) % 4, (q + dq) % 4
        return at(p_ + core * (q_ - p_), q_ + core * (p_ - q_), z, core)

    def at_z(d, y_=y):
        return at(x, y_, (z + d + 16) % 16, core)

    def signal(sem, dev):
        pl.semaphore_signal(sem, inc=1, device_id=dev, device_id_type=MESH)

    sib = at(x, y, z, 1 - core)

    def same(x_, y_):
        return (x == x_) & (y == y_)

    gives = [(y < 2) & jnp.logical_not(same(2 * y + n, x)) for n in range(2)]
    keeps = [(y < 2) & same(2 * y + n, x) for n in range(2)]
    gets = jnp.logical_not(same(y, x // 2))

    barrier = pltpu.get_barrier_semaphore()
    partners = [sib] + [at_pq(d, 0) for d in (1, 2, 3)] + [at_pq(0, d) for d in (1, 2, 3)]
    partners += [at_z(d) for d in NEAR_Z]
    for dev in partners:
        signal(barrier, dev)

    @pl.when(gets)
    def _():
        signal(barrier, at(y, x // 2, z, core))

    for copy in loads:
        copy.wait()

    wide = a_ref[...].astype(F32)
    spread = jnp.sqrt(jnp.sum(wide * wide, axis=0, keepdims=True) * INV + 1e-06)
    e = jnp.full_like(spread, 2.0**10)
    for k in range(-9, 5):
        e = jnp.where(spread >= 2.0**k, 2.0**-k, e)
    se = spread * e
    factor = 1.0 / (se * se * se * e)
    scaled = wide * e
    narrow = scaled.astype(BF16)
    line = lax.broadcasted_iota(jnp.int32, (16, 128), 0)
    zero = jnp.zeros((16, 128), F32)
    halves = []
    for h in range(2):
        rows = zero
        for n, part in enumerate(split_three(factor[:, h * 128:h * 128 + 128])):
            rows = jnp.where(line == h * 8 + n, part, rows)
        halves.append(rows)

    for n in range(2):
        imsg[n, 0:128] = narrow[:, n * 128:n * 128 + 128]
        imsg[n, 128:144] = halves[n].astype(BF16)

        @pl.when(keeps[n])
        def _():
            ibuf[0] = imsg[n]


    jbuf[0, 0:256, :] = scaled.T.astype(BF16)
    jbuf[0, 256:320, :] = v_ref[:, 0:128]
    jbuf[0, 320:384, :] = v_ref[:, 128:256]
    jbuf[0, 384:400, :] = (halves[0] + halves[1]).astype(BF16)

    pl.semaphore_wait(barrier, len(partners) + sum(g.astype(jnp.int32) for g in gives))

    sent = []

    def remote(src, dst, recv, dev):
        copy = pltpu.make_async_remote_copy(
            src_ref=src, dst_ref=dst, send_sem=send_sem.at[len(sent)], recv_sem=recv,
            device_id=dev, device_id_type=MESH,
        )
        sent.append(copy)
        return copy

    def send(*args):
        remote(*args).start()

    def arrived(dst, recv):
        pltpu.make_async_remote_copy(
            src_ref=dst, dst_ref=dst, send_sem=misc.at[0], recv_sem=recv,
            device_id=sib, device_id_type=MESH,
        ).wait_recv()

    def ichunk(slot):
        return ibuf.at[slot, 0:128]

    def isend(k, d):
        dst = (k - d) % 16
        send(ichunk(k % 16), ichunk(dst), irecv.at[dst], at_z(d))

    def iwait(*ks):
        for k in ks:
            arrived(ichunk(k % 16), irecv.at[k % 16])

    started = []

    def send_if(cond, *args):
        copy = remote(*args)
        sent[-1] = None
        pl.when(cond)(copy.start)
        started.append((copy, cond))

    def jsend(src, dst, dev):
        send(jbuf.at[src], jbuf.at[dst], jrecv.at[dst], dev)

    def jwait(n):
        arrived(jbuf.at[n], jrecv.at[n])

    def to_sib(n):
        jsend(n, 16 + n, sib)

    def along_q(dp):
        for d in (1, 3) if dp % 2 else (1, 3, 2):
            jsend(SLOT[dp, 0], SLOT[dp, 4 - d], at_pq(0, d))

    def across_q(dp):
        jsend(SLOT[dp, 1], SLOT[dp, 2], at_pq(0, 3))

    def prep(n):
        rows = jbuf[n, 384:400, :].astype(F32)
        for h in range(2):
            f = jnp.sum(rows[h * 8:h * 8 + 8, :], axis=0, keepdims=True)
            w = jbuf[n, 256 + h * 64:320 + h * 64, :].astype(F32) * f
            hi = w.astype(BF16)
            lo = (w - hi.astype(F32)).astype(BF16)
            lanes = slice(n * 256 + h * 128, n * 256 + h * 128 + 128)
            vbuf[0:64, lanes] = hi
            vbuf[64:128, lanes] = lo

    for n in range(2):
        send_if(gives[n], imsg.at[n], ibuf.at[0], irecv.at[0], at((2 * y + n) % 4, x, z, core))
    for d in (1, 3, 2):
        jsend(0, SLOT[4 - d, 0], at_pq(d, 0))
    along_q(0)
    to_sib(0)

    @pl.when(gets)
    def _():
        arrived(ibuf.at[0], irecv.at[0])

    for d in NEAR_Z:
        isend(0, d)
    for d in (3, -3):
        signal(zsem, at_z(d))
    prep(0)

    def tile(groups, chunks):
        weights = jnp.concatenate(chunks, axis=1)
        total = None
        for first, n in groups:
            states = jbuf[first:first + n, 0:256, :].reshape(n * 256, 128)
            prod = dot(states, weights)
            square = prod * prod
            local = (square * square).astype(BF16)
            part = dot(vbuf[:, first * 256:(first + n) * 256], local)
            total = part if total is None else total + part
        return total[0:64, :] + total[64:128, :]

    def add_tiles(groups, ks, fresh):
        total = tile(groups, [ibuf[k % 16, 0:128] for k in ks])
        for n, k in enumerate(ks):
            part = total[:, n * 128:n * 128 + 128]
            acc[k % 16] = part if fresh else acc[k % 16] + part

    def take(*offs):
        for off in offs:
            jwait(SLOT[off])
            to_sib(SLOT[off])

    for dp in (1, 3):
        take((dp, 0))
        along_q(dp)
    take((0, 1), (0, 3))
    take((2, 0))
    along_q(2)
    pl.semaphore_wait(zsem, 2)
    for d in (5, -5):
        signal(wsem, at_z(d))
    iwait(-3)
    for d in (3, 1, 2):
        isend(-3, d)
    iwait(3)
    for d in (-3, -1, -2):
        isend(3, d)
    for n in range(1, 5):
        prep(n)
    for n in range(16, 21):
        jwait(n)
        prep(n)
    for dp in (1, 3):
        take((dp, 1), (dp, 3))
        across_q(dp)
    iwait(-1, 1, -2, 2)
    add_tiles(FIRST, [0, 1, -1, 2, -2, 3, -3], True)
    take((0, 2))

    pl.semaphore_wait(wsem, 2)
    signal(xsem, at(x + 1 - 2 * (x % 2), y, z, core))
    for n in range(5, 11):
        prep(n)
    iwait(-6)
    isend(-6, 2)
    isend(-6, 1)
    iwait(6)
    isend(6, -1)
    pl.semaphore_wait(xsem, 1)
    signal(csem, sib)
    for n in range(21, 27):
        jwait(n)
        prep(n)
    take((2, 1), (2, 3))
    take((1, 2), (3, 2), (2, 2))
    iwait(-4, 4, -5, 5)
    add_tiles(FIRST, [4, -4, 5, -5, 6, -6], True)
    for n in range(11, 16):
        prep(n)
    for n in range(27, 32):
        jwait(n)
        prep(n)
    pl.semaphore_wait(csem, 1)

    def deliver(src, dst, recv, zs):
        bit, h = x % 2, (zs // 2) % 2
        dx, dz, dc = x - bit + (zs // 4) % 2, 8 * h + 4 * (zs // 8) + 2 * core + bit, zs % 2
        mine = (dx == x) & (dz == z) & (dc == core)
        send_if(jnp.logical_not(mine), src, dst, recv, at(dx, y, dz, dc))
        pl.when(mine)(pltpu.make_async_copy(src, dst, recv).start)

    deliver(ibuf.at[0, 128:144], fto, misc.at[3], z)

    iwait(7, -7, 8)
    add_tiles(FIRST, [7, -7, 8], True)
    near = ((z - 2 * core - x % 2 + 18) // 4) % 4
    for step in range(4):
        g = sum((near == n).astype(jnp.int32) * turn[step] for n, turn in enumerate(TURNS))
        h, zs_hi = g // 2, g % 2
        begins = [8 * zs_hi + 4 * a + 2 * h + b for a in range(2) for b in range(2)]
        rels = [(zs - z + 16) % 16 for zs in begins]
        total = tile(REST, [ibuf[rel, 0:128] for rel in rels])
        for n, rel in enumerate(rels):
            outbox[4 * step + n] = (acc[rel] + total[:, n * 128:n * 128 + 128]).astype(BF16)
        for n in range(4):
            deliver(outbox.at[4 * step + n], inbox.at[z], rrecv.at[z], begins[n])

    result = None
    arrived(fto, misc.at[3])
    for n in range(16):
        arrived(inbox.at[n], rrecv.at[n])
    for n in range(16):
        part = inbox[n].astype(F32)
        result = part if result is None else result + part
    o_ref[...] = result * (jnp.sum(fto[...].astype(F32), axis=0, keepdims=True) * INV**4)

    for copy in sent:
        if copy is not None:
            copy.wait_send()
    for copy, cond in started:
        pl.when(cond)(copy.wait_send)


def per_device(anomalies, vectors):
    vmem, hbm = pl.BlockSpec(memory_space=pltpu.VMEM), pl.BlockSpec(memory_space=pl.ANY)
    return pl.pallas_call(
        kernel,
        out_shape=jax.ShapeDtypeStruct((VECS, 128), F32),
        in_specs=[hbm, hbm],
        out_specs=vmem,
        scratch_shapes=[
            pltpu.VMEM((MEMBERS, 256), BF16),
            pltpu.VMEM((VECS, 256), BF16),
            pltpu.VMEM((32, JROWS, 128), BF16),
            pltpu.VMEM((128, 8192), BF16),
            pltpu.VMEM((16, IROWS, 128), BF16),
            pltpu.VMEM((2, IROWS, 128), BF16),
            pltpu.VMEM((16, 128), BF16),
            pltpu.VMEM((16, VECS, 128), F32),
            pltpu.VMEM((16, VECS, 128), BF16),
            pltpu.VMEM((16, VECS, 128), BF16),
            pltpu.SemaphoreType.DMA((80,)),
            pltpu.SemaphoreType.DMA((32,)),
            pltpu.SemaphoreType.DMA((16,)),
            pltpu.SemaphoreType.DMA((16,)),
            pltpu.SemaphoreType.DMA((4,)),
        ] + [pltpu.SemaphoreType.REGULAR] * 4,
        compiler_params=pltpu.CompilerParams(
            collective_id=0, has_side_effects=True, vmem_limit_bytes=48 * 2**20
        ),
    )(anomalies, vectors)


def solution(mesh):
    return jax.shard_map(
        per_device,
        mesh=mesh,
        in_specs=(P(None, ("col", "row")), P(None, ("col", "row"))),
        out_specs=P(None, ("row", "col")),
        check_vma=False,
    )
```
